32 devices in a mesh: fsdp: 8 (over z, y), dom: 4 (over x, core).
Axes of the slice: x: 2, y: 2, z: 4, core: 2. Of those that a mesh axis runs over, the one named last changes fastest.
Arguments:
- tokens: bfloat16 [8192, 8192], P(('fsdp', 'dom')), may hold values from -6 to 6
- key_grad: bfloat16 [8192, 512], P(('fsdp', 'dom')), may hold values from -6 to 6
- weight: bfloat16 [8192, 512], P('fsdp'), may hold values from -0.0625 to 0.0625
- master: float32 [8192, 512], P(('fsdp', 'dom')), may hold values from -0.0625 to 0.0625
- moment_one: float32 [8192, 512], P(('fsdp', 'dom')), may hold values from -3 to 3
- moment_two: float32 [8192, 512], P(('fsdp', 'dom')), may hold values from 0.1 to 4
- live: int32 [8, 4], replicated, may hold values from 0 to 1, as said below
- buddy: int32 [4], replicated, may hold values from 0 to 3, as said below
Outputs:
- keys: bfloat16 [8192, 512], P(('fsdp', 'dom'))
- input_grad: bfloat16 [8192, 8192], P(('fsdp', 'dom'))
- new_weight: bfloat16 [8192, 512], P('fsdp')
- new_master: float32 [8192, 512], P(('fsdp', 'dom'))
- new_one: float32 [8192, 512], P(('fsdp', 'dom'))
- new_two: float32 [8192, 512], P(('fsdp', 'dom'))
- held_copy: float32 [3, 8192, 512], P(None, ('fsdp', 'dom'))
The draws below stay inside these ranges and needn't reach their ends.
Inputs may be any that keep to these rules, and one draw needn't show every extreme that they name: `live`: every column (domain) has at least one 1. A permutation of the domains in a single cycle; no domain is its own buddy; some domain's buddy lies 4 / 2 domains further round.
All inputs are finite; a program needn't handle non-finite values.
Results may differ from the reference program's by a relative error of at most 0.005.
Values may be sent and summed in bfloat16 or wider, within the bound.
No kernel may reach another device: no remote copies, remote signals or barrier semaphores. Data moves between devices by JAX's collectives and lax.ppermute only.
A program may use at most 128 MiB of HBM per device.

```python
import math
import jax
import jax.numpy as jnp
from jax import lax

D = 8192
TOK_DEV = 256
STEP = 100
KD = 512
FSDPS = 8
DOMS = 4
TOKENS = 8192


def draw_live(key, part):
    picks = jax.random.randint(jax.random.fold_in(key, 11), (FSDPS, DOMS), 0, 4)
    alive = (picks > 0).astype(jnp.int32)
    keeper = jax.random.randint(jax.random.fold_in(key, 12), (DOMS,), 0, FSDPS)
    forced = (jnp.arange(FSDPS)[:, None] == keeper[None, :]).astype(jnp.int32)
    return jnp.maximum(alive, forced).astype(jnp.int32)


def draw_buddy(key, part):
    shuffled = jax.random.permutation(jax.random.fold_in(key, 13), DOMS).astype(jnp.int32)
    first = jax.random.randint(jax.random.fold_in(key, 14), (), 0, DOMS).astype(jnp.int32)
    second = ((first + DOMS // 2) % DOMS).astype(jnp.int32)
    values = jnp.arange(DOMS, dtype=jnp.int32)
    place = jnp.zeros((DOMS,), jnp.int32).at[shuffled].set(values)
    score = jnp.where(values == first, -2, jnp.where(values == second, -1, place)).astype(jnp.int32)
    order = jnp.argsort(score, stable=True).astype(jnp.int32)
    return jnp.zeros((DOMS,), jnp.int32).at[order].set(jnp.roll(order, -1)).astype(jnp.int32)


def with_spikes(entries, own_key, source, target, shards_of, factor):
    def block_of(dim):
        return (jnp.arange(entries.shape[dim]) // (entries.shape[dim] // shards_of)).reshape((-1,) + (1,) * (entries.ndim - 1 - dim))

    one_side = jax.random.permutation(own_key, shards_of)[block_of(target)]
    far = (block_of(target) + shards_of // 2) % shards_of
    return jnp.where((block_of(source) == one_side) | (block_of(source) == far), factor * entries, entries)


def steps_of(rng, extent, split, low, top_value):
    def one(dim, parts):
        draws = jax.random.uniform(jax.random.fold_in(jax.random.fold_in(rng, 6), dim), (parts,), jnp.float32, low / len(split), top_value / len(split))
        return jnp.repeat(jnp.exp(draws), extent[dim] // parts).reshape((-1,) + (1,) * (len(extent) - dim - 1))

    loudness = one(*split[0])
    for cut in split[1:]:
        loudness = loudness * one(*cut)
    return loudness


def scatter_about(key, extent, width, bound, cuts=(), held_as=jnp.bfloat16):
    drawn = jax.random.normal(key, extent, jnp.float32) * width
    if len(cuts) > 0:
        drawn = steps_of(key, extent, cuts, -0.22, 0.18) * drawn
    return jnp.clip(drawn, min=-bound, max=bound).astype(held_as)


def gaussian_with(key, shape, spread, reach, split, heavy, kind=jnp.bfloat16):
    array = spread * jax.random.normal(key, shape, jnp.float32)
    if split:
        array = array * steps_of(key, shape, split, -0.22, 0.18)
    return jnp.clip(with_spikes(array, jax.random.fold_in(key, 3), *heavy), -reach, reach).astype(kind)


def setup_inputs(seed: int = 0) -> dict:
    key_of = jax.random.split(jax.random.key(seed), 9)
    tokens = gaussian_with(key_of[0], (TOKENS, D), 1.0, 6.0, ((0, 32),), (0, 1, 32, 2.75))
    key_grad = scatter_about(key_of[1], (TOKENS, KD), 1.0, 6.0, ((0, 32),))
    weight = scatter_about(key_of[2], (D, KD), D ** -0.5, 0.0625, ((0, 8),))
    master = scatter_about(key_of[3], (D, KD), D ** -0.5, 0.0625, ((0, 32),), jnp.float32)
    moment_one = scatter_about(key_of[4], (D, KD), 0.5, 3.0, ((0, 32),), jnp.float32)
    moment_two = jnp.clip(jnp.exp(math.log(4.0) - 3.6888794 * jax.random.uniform(key_of[5], (D, KD), jnp.float32) ** steps_of(key_of[5], (D, KD), ((0, 32),), -0.2, 0.2)), 0.1, 4.0)
    live = draw_live(jax.random.fold_in(key_of[8], 71), 0)
    buddy = draw_buddy(jax.random.fold_in(key_of[8], 71), 0)
    return dict(tokens=tokens, key_grad=key_grad, weight=weight, master=master, moment_one=moment_one, moment_two=moment_two, live=live, buddy=buddy)


def reference(tokens, key_grad, weight, master, moment_one, moment_two, live, buddy):
    devs = FSDPS * DOMS
    live_flat = live.reshape(-1).astype(jnp.float32)
    total = jnp.sum(live_flat)
    scales = live_flat * devs / (total * TOK_DEV)
    blocks = tokens.reshape(devs, TOK_DEV, D)
    cotans = key_grad.reshape(devs, TOK_DEV, KD)

    def step(carry, item):
        block, cotan, scale = item
        xf = block.astype(jnp.float32)
        rstd = lax.rsqrt(lax.optimization_barrier(jnp.mean(xf * xf, axis=1, keepdims=True)) + 1e-05)
        hat = xf * rstd
        normed = hat.astype(jnp.bfloat16)
        keys = jnp.dot(normed, weight, preferred_element_type=jnp.float32).astype(jnp.bfloat16)
        back = lax.dot_general(cotan, weight, (((1,), (1,)), ((), ())), preferred_element_type=jnp.float32)
        dx = (rstd * (back - hat * lax.optimization_barrier(jnp.mean(back * hat, axis=1, keepdims=True)))).astype(jnp.bfloat16)
        term = lax.dot_general(normed, cotan, (((0,), (0,)), ((), ())), preferred_element_type=jnp.float32)
        return (carry + term * scale, (keys, dx))
    grad, (keys, dx) = lax.scan(step, jnp.zeros((D, KD), jnp.float32), (blocks, cotans, scales))
    new_one = 0.9 * moment_one + 0.1 * grad
    new_two = 0.95 * moment_two + 0.05 * grad * grad
    first = 1.0 - 0.9 ** STEP
    second = 1.0 - 0.95 ** STEP
    update = new_one / first / (jnp.sqrt(new_two / second) + 1e-08)
    new_master = master - 0.002 * (update + 0.1 * master)
    new_weight = new_master.astype(jnp.bfloat16)
    inverse = jnp.zeros((DOMS,), jnp.int32).at[buddy].set(jnp.arange(DOMS, dtype=jnp.int32))
    rows = D // devs
    stacked = jnp.stack((new_master, new_one, new_two)).reshape(3, FSDPS, DOMS, rows, KD)
    held = jnp.take(stacked, inverse, axis=2).reshape(3, D, KD)
    return (keys.reshape(TOKENS, KD), dx.reshape(TOKENS, D), new_weight, new_master, new_one, new_two, held)
```

```python
import jax
import jax.numpy as jnp
from jax import lax
from jax.experimental import pallas as pl
from jax.experimental.pallas import tpu as pltpu
from jax.sharding import Mesh
from jax.sharding import PartitionSpec as P

STEP = 100


def shift(value, axis, by):
    size = lax.axis_size(axis)
    return lax.ppermute(value, axis, [(i, (i + by) % size) for i in range(size)])


def pick(array, index, dim):
    return lax.dynamic_index_in_dim(array, index, dim, keepdims=False)


def scatter_sum(terms, axis, dim):
    size = lax.axis_size(axis)
    here = lax.axis_index(axis)
    arrived = [
        shift(pick(terms, (here + by) % size, dim).astype(jnp.bfloat16), axis, by)
        for by in range(1, size)
    ]
    total = pick(terms, here, dim)
    for term in arrived:
        total = total + term.astype(jnp.float32)
    return total


def gather(value, axis, dim):
    size = lax.axis_size(axis)
    here = lax.axis_index(axis)
    if size == 2:
        other = shift(value, axis, 1)
        first = jnp.where(here == 0, value, other)
        second = jnp.where(here == 0, other, value)
        return jnp.stack((first, second), axis=dim)
    slots = jnp.zeros(value.shape[:dim] + (size,) + value.shape[dim:], value.dtype)
    for by in range(size):
        arrived = shift(value, axis, by) if by else value
        slots = lax.dynamic_update_index_in_dim(slots, arrived, (here - by) % size, dim)
    return slots


def general(tokens, key_grad, weight, master, moment_one, moment_two, live, buddy):
    planes, rows_of, chips, cores = (lax.axis_size(a) for a in ("z", "y", "x", "c"))
    z, y, x, c = (lax.axis_index(a) for a in ("z", "y", "x", "c"))
    member = z * rows_of + y
    domain = x * cores + c
    rows, width = master.shape
    half = rows // 2
    features = tokens.shape[1]

    xf = tokens.astype(jnp.float32)
    rstd = lax.rsqrt(jnp.mean(xf * xf, axis=1, keepdims=True) + 1e-05)
    hat = xf * rstd
    normed = hat.astype(jnp.bfloat16)

    quarter = pick(pick(weight.reshape(chips, cores, rows, width), x, 0), c, 0)
    column = gather(quarter, "z", 0)
    upper = gather(gather(column[:, :half], "y", 1), "x", 2)
    lower = gather(gather(column[:, half:], "x", 1), "y", 1)
    mine = jnp.concatenate((upper, lower), axis=3)
    whole = gather(mine, "c", 3).reshape(features, width)

    live_float = live.astype(jnp.float32)
    norming = live.shape[0] * live.shape[1] / (jnp.sum(live_float) * tokens.shape[0])
    alive_here = pick(pick(live_float, member, 0), domain, 0)
    scale = alive_here * norming
    product = lax.dot_general(
        normed, key_grad, (((0,), (0,)), ((), ())), preferred_element_type=jnp.float32
    )
    terms = (product * scale).reshape(planes, rows_of, chips, cores, rows, width)
    terms = scatter_sum(terms, "c", 3)
    upper_sum = scatter_sum(scatter_sum(terms[:, :, :, :half], "x", 2), "y", 1)
    lower_sum = scatter_sum(scatter_sum(terms[:, :, :, half:], "y", 1), "x", 1)
    grad = scatter_sum(jnp.concatenate((upper_sum, lower_sum), axis=1), "z", 0)

    new_one = 0.9 * moment_one + 0.1 * grad
    new_two = 0.95 * moment_two + 0.05 * grad * grad
    first = 1.0 - 0.9**STEP
    second = 1.0 - 0.95**STEP
    update = new_one / first / (jnp.sqrt(new_two / second) + 1e-08)
    new_master = master - 0.002 * (update + 0.1 * master)

    state = jnp.stack((new_master, new_one, new_two)).astype(jnp.bfloat16)
    states = gather(state, "x", 0)
    new_weight = gather(states[:, 0], "c", 1).reshape(weight.shape)
    slots = jnp.arange(chips * cores, dtype=jnp.int32)
    source = jnp.sum(slots * (buddy == domain).astype(jnp.int32))
    other_source = jnp.sum(slots * (buddy == x * cores + 1 - c).astype(jnp.int32))
    from_core = shift(pick(states, other_source // cores, 0), "c", 1)
    from_column = pick(states, source // cores, 0)
    held = jnp.where(source % cores == c, from_column, from_core).astype(jnp.float32)

    keys = jnp.dot(normed, whole, preferred_element_type=jnp.float32)
    inner = jnp.sum(key_grad.astype(jnp.float32) * keys, axis=1, keepdims=True) / features
    back = lax.dot_general(
        key_grad, whole, (((1,), (1,)), ((), ())), preferred_element_type=jnp.float32
    )
    input_grad = (rstd * (back - hat * inner)).astype(jnp.bfloat16)
    return (keys.astype(jnp.bfloat16), input_grad, new_weight, new_master, new_one, new_two, held)


VMEM = pl.BlockSpec(memory_space=pltpu.VMEM)
SMEM = pl.BlockSpec(memory_space=pltpu.SMEM)
MIB = 2**20


def local(body, outs, flops, traffic, limit, *operands, scalars=0, **more):
    return pl.pallas_call(
        body,
        out_shape=[jax.ShapeDtypeStruct(s, t) for s, t in outs],
        in_specs=[SMEM] * scalars + [VMEM] * (len(operands) - scalars),
        out_specs=[VMEM] * len(outs),
        cost_estimate=pl.CostEstimate(flops=8, bytes_accessed=8, transcendentals=0),
        compiler_params=pltpu.CompilerParams(vmem_limit_bytes=limit * MIB),
        **more,
    )(*operands)


def after(value, *others):
    return lax.optimization_barrier((value, *others))[0]


def place():
    return tuple(lax.axis_index(a) for a in ("z", "y", "x", "c"))


def block_of(planes, by, flip_y, flip_x):
    z, y, x, _ = place()
    z = lax.rem(z + (by + planes) % planes, planes)
    return (z * 2 + (1 - y if flip_y else y)) * 2 + (1 - x if flip_x else x)


def prepare_body(rows, order, tokens, ours, soon, later, rstd_out, held, sems):
    c = lax.axis_index("c")
    many, features = tokens.shape
    step = many // 8

    def rows_in(i):
        span = pl.ds(pl.multiple_of(i * step, step), step)
        return pltpu.make_async_copy(tokens.at[span], held.at[span], sems.at[i])

    for i in range(8):
        rows_in(i).start()
    places = [(by, fy, fx) for by in order for fy in (0, 1) for fx in (0, 1)]

    def part(i, _):
        rows_in(i).wait()
        span = pl.ds(pl.multiple_of(i * step, step), step)
        squares = jnp.zeros((step, 128), jnp.float32)
        for j in range(0, features, 512):
            some = held[span, j : j + 512].astype(jnp.float32)
            some = some * some
            for k in range(0, 512, 128):
                squares = squares + some[:, k : k + 128]
        mean = jnp.sum(squares, axis=1, keepdims=True) / features
        rstd = lax.rsqrt(mean + 1e-05)
        rstd_out[span] = rstd
        for side, outs in ((1 - c, (soon, later)), (c, (ours,))):
            share = len(places) // len(outs)
            for j, flips in enumerate(places):
                start = (block_of(len(order), *flips) * 2 + side) * rows
                columns = pl.ds(pl.multiple_of(start, rows), rows)
                at = j % share * rows
                outs[j // share][span, at : at + rows] = (
                    held[span, columns].astype(jnp.float32) * rstd
                ).astype(jnp.bfloat16)
        return 0

    lax.fori_loop(0, 8, part, 0)


def prepare(tokens, rows, order):
    many, features = tokens.shape
    side = ((many, features // 2), jnp.bfloat16)
    part = ((many, features // 4), jnp.bfloat16)
    return pl.pallas_call(
        lambda *refs: prepare_body(rows, order, *refs),
        out_shape=[jax.ShapeDtypeStruct(s, t) for s, t in (side, part, part, ((many, 1), jnp.float32))],
        in_specs=[pl.BlockSpec(memory_space=pltpu.HBM)],
        out_specs=[VMEM] * 4,
        scratch_shapes=[pltpu.VMEM(tokens.shape, tokens.dtype), pltpu.SemaphoreType.DMA((8,))],
        cost_estimate=pl.CostEstimate(flops=8, bytes_accessed=8, transcendentals=0),
        compiler_params=pltpu.CompilerParams(vmem_limit_bytes=47 * MIB),
    )(tokens)


def flags_body(many, live, flags):
    z, y, x, c = place()
    for row, core in ((0, c), (8, 1 - c)):
        alive = live[x * 2 + core, z * 2 + y]
        flags[row : row + 8] = jnp.full((8, flags.shape[1]), alive).astype(jnp.float32)
    blocks = live.shape[0] * live.shape[1]
    alive = sum(live[i, j] for i in range(live.shape[0]) for j in range(live.shape[1]))
    flags[16:24] = blocks / (jnp.full((8, flags.shape[1]), alive).astype(jnp.float32) * many)


def product(order, by, flip_y, flip_x, lower, rows, cores):
    half = rows // 2
    start = (order.index(by) * 4 + flip_y * 2 + flip_x) * rows + lower * half

    def term(parts, grad, flag):
        share = len(order) * 4 * rows // len(parts)
        at = start % share
        return flag * lax.dot_general(
            parts[start // share][:, at : at + half],
            grad[...],
            (((0,), (0,)), ((), ())),
            preferred_element_type=jnp.float32,
        )

    return sum(term(*core) for core in cores)


def first_body(order, rows, group, flags, ours, theirs, own_grad, their_grad, to_x, to_y):
    cores = (((ours,), own_grad, flags[0:1]), ((theirs, theirs), their_grad, flags[8:9]))
    for i, by in enumerate(group):
        for flip in (0, 1):
            to_x[flip, i] = product(order, by, flip, 1, 0, rows, cores).astype(jnp.bfloat16)
            to_y[flip, i] = product(order, by, 1, flip, 1, rows, cores).astype(jnp.bfloat16)


def second_body(order, rows, group, flags, ours, soon, later, own_grad, their_grad, from_x, from_y, to_y, to_x):
    cores = (((ours,), own_grad, flags[0:1]), ((soon, later), their_grad, flags[8:9]))
    for i, by in enumerate(group):
        upper = product(order, by, 1, 0, 0, rows, cores)
        to_y[i] = (upper + from_x[1, i].astype(jnp.float32)).astype(jnp.bfloat16)
        lower = product(order, by, 0, 1, 1, rows, cores)
        to_x[i] = (lower + from_y[1, i].astype(jnp.float32)).astype(jnp.bfloat16)


def own_half(order, rows, by, i, lower, cores, near, second):
    total = product(order, by, 0, 0, lower, rows, cores)
    return total + near[0, i].astype(jnp.float32) + second[i].astype(jnp.float32)


def third_body(order, rows, group, flags, ours, soon, later, own_grad, their_grad, from_x, from_y, late_y, late_x, *outs):
    cores = (((ours,), own_grad, flags[0:1]), ((soon, later), their_grad, flags[8:9]))
    half = rows // 2
    for i, by in enumerate(group):
        upper = own_half(order, rows, by, i, 0, cores, from_x, late_y)
        lower = own_half(order, rows, by, i, 1, cores, from_y, late_x)
        outs[i][:half] = upper.astype(jnp.bfloat16)
        outs[i][half:] = lower.astype(jnp.bfloat16)


def stepped(grad, master, moment_one, moment_two):
    one = 0.9 * moment_one + 0.1 * grad
    two = 0.95 * moment_two + 0.05 * grad * grad
    first = 1.0 - 0.9**STEP
    second = 1.0 - 0.95**STEP
    update = one / first / (jnp.sqrt(two / second) + 1e-08)
    return master - 0.002 * (update + 0.1 * master), one, two


def state_body(order, rows, at, flags, ours, soon, later, own_grad, their_grad, from_x, from_y, late_y, late_x, master, moment_one, moment_two, *rest):
    *along_z, state, grad = rest
    cores = (((ours,), own_grad, flags[0:1]), ((soon, later), their_grad, flags[8:9]))
    half = rows // 2
    for lower, near, second in ((0, from_x, late_y), (1, from_y, late_x)):
        total = own_half(order, rows, 0, at, lower, cores, near, second)
        span = pl.ds(lower * half, half)
        for term in along_z:
            total = total + term[span].astype(jnp.float32)
        total = total * flags[16:17]
        grad[span] = total
        for i, value in enumerate(stepped(total, master[span], moment_one[span], moment_two[span])):
            state[i, span] = value.astype(jnp.bfloat16)


def update_body(grad, master, moment_one, moment_two, new_master, new_one, new_two):
    new_master[...], new_one[...], new_two[...] = stepped(
        grad[...], master[...], moment_one[...], moment_two[...]
    )


def piece_columns(planes, rows, by, flip_y, flip_x, flip_c):
    c = lax.axis_index("c")
    block = block_of(planes, -by, flip_y, flip_x)
    return pl.ds(pl.multiple_of((block * 2 + (1 - c if flip_c else c)) * rows, rows), rows)


def normed_at(tokens, span, rstd):
    return (tokens[:, span].astype(jnp.float32) * rstd).astype(jnp.bfloat16)


def each(where, pieces):
    for blocks, piece in zip(where, pieces):
        for k, at in enumerate(blocks):
            yield at, piece.at[k]


def add_keys(planes, rows, where, tokens, rstd, pieces, keys):
    for blocks, piece in zip(where, pieces):
        normed = [normed_at(tokens, piece_columns(planes, rows, *at), rstd) for at in blocks]
        deep = piece[...].reshape(-1, piece.shape[2])
        keys = keys + jnp.dot(
            jnp.concatenate(normed, axis=1), deep, preferred_element_type=jnp.float32
        )
    return keys


def back_of(key_grad, piece):
    return lax.dot_general(
        key_grad[...], piece[...], (((1,), (1,)), ((), ())), preferred_element_type=jnp.float32
    )


def both_ways_body(planes, rows, where, tokens, key_grad, rstd_in, *rest):
    pieces = rest[: len(where)]
    keys_out, input_grad, made, sems = rest[len(where) :]
    features = tokens.shape[1]
    rstd = rstd_in[...]
    keys = jnp.zeros(key_grad.shape, jnp.float32)
    keys = add_keys(planes, rows, where, tokens, rstd, pieces, keys)
    keys_out[...] = keys.astype(jnp.bfloat16)
    inner = jnp.sum(key_grad[...].astype(jnp.float32) * keys, axis=1, keepdims=True) / features
    slope = jnp.broadcast_to(rstd * rstd * inner, (tokens.shape[0], rows))
    found = dict(each(where, pieces))
    copies = []
    for i, (fy, by) in enumerate((fy, by) for fy in (0, 1) for by in range(planes)):
        for at in ((by, fy, fx, fc) for fx in (0, 1) for fc in (0, 1)):
            span = piece_columns(planes, rows, *at)
            back = rstd * back_of(key_grad, found[at])
            made[:, span] = (back - tokens[:, span].astype(jnp.float32) * slope).astype(jnp.bfloat16)
        start = block_of(planes, -by, fy, 0) // 2 * (4 * rows)
        span = pl.ds(pl.multiple_of(start, rows), 4 * rows)
        copies.append(pltpu.make_async_copy(made.at[:, span], input_grad.at[:, span], sems.at[i]))
        copies[-1].start()
    for copy in copies:
        copy.wait()


def quarter_body(rows, weight, out):
    _, _, x, c = place()
    out[...] = weight[pl.ds(pl.multiple_of((x * 2 + c) * rows, rows), rows)]


def stack_body(*refs):
    *parts, out = refs
    for i, part in enumerate(parts):
        out[i] = part[...]


def finish_body(rows, buddy, own, beside, across, diagonal, new_weight, held):
    _, _, x, c = place()
    domain = x * 2 + c
    for flip_x, flip_c, state in ((0, 0, own), (0, 1, beside), (1, 0, across), (1, 1, diagonal)):
        sender = (1 - x if flip_x else x) * 2 + (1 - c if flip_c else c)
        new_weight[pl.ds(pl.multiple_of(sender * rows, rows), rows)] = state[0]

        @pl.when(buddy[sender] == domain)
        def _():
            held[...] = state[...].astype(jnp.float32)


def on_device(tokens, key_grad, weight, master, moment_one, moment_two, live, buddy):
    planes, rows_of, chips, cores = (lax.axis_size(a) for a in ("z", "y", "x", "c"))
    rows, width = master.shape
    many, features = tokens.shape
    if (rows_of, chips, cores) != (2, 2, 2) or rows % 256 or many % 128 or planes < 2 or width != 512:
        return general(tokens, key_grad, weight, master, moment_one, moment_two, live, buddy)
    half = rows // 2
    low, full = jnp.bfloat16, jnp.float32
    live = live.T
    order = sorted(range(1, planes), key=lambda by: min(by, planes - by)) + [0]

    def simple(body, outs, *operands, limit=12, **more):
        return local(body, outs, 8, 8, limit, *operands, **more)

    quarter, = simple(lambda *refs: quarter_body(rows, *refs), [((rows, width), low)], weight)
    opposite = lax.ppermute(quarter, ("y", "x"), [(0, 3), (1, 2), (2, 1), (3, 0)])
    quarters, opposites = [quarter], [opposite]
    for by in range(1, planes):
        quarters.append(shift(quarters[-1], "z", 1))
        opposites.append(shift(opposites[-1], "z", 1))
    column, = simple(
        stack_body,
        [((planes, rows, width), low)],
        *quarters,
    )
    corner, = simple(stack_body, [((planes, rows, width), low)], *opposites)

    ours, soon, later, rstd = prepare(tokens, rows, order)
    flags, = simple(
        lambda *refs: flags_body(many, *refs),
        [((24, width), full)],
        after(live, soon),
        scalars=1,
    )
    grads = key_grad, shift(after(key_grad, soon), "c", 1)
    theirs = shift(soon, "c", 1), shift(after(later, grads[1]), "c", 1)
    cores = (flags, ours, *theirs, *grads)

    groups = order[: planes // 2], order[planes // 2 :]
    came = []
    for group, part in zip(groups, theirs):
        to_x, to_y = simple(
            lambda *refs: first_body(order, rows, group, *refs),
            [((2, len(group), half, width), low)] * 2,
            flags, ours, part, *grads,
        )
        came.append((shift(to_x, "x", 1), shift(to_y, "y", 1)))
    late = []
    along_z = []
    first_out = ()
    for group, (from_x, from_y), ties in zip(groups, came, ((), quarters[1:3])):
        to_y, to_x = simple(
            lambda *refs: second_body(order, rows, group, *refs),
            [((len(group), half, width), low)] * 2,
            *cores, after(from_x, *(late_out if along_z else ())), after(from_y, *ties),
        )
        late_out = (to_y, to_x)
        late.append((shift(to_y, "y", 1), shift(to_x, "x", 1)))
        sent = [by for by in group if by]
        to_z = simple(
            lambda *refs: third_body(order, rows, sent, *refs),
            [((rows, width), low)] * len(sent),
            *cores, from_x, from_y, after(late[-1][0], *(first_out or (*quarters[3:], opposites[1]))), late[-1][1],
        )
        first_out = to_z
        along_z += [shift(term, "z", by) for by, term in zip(sent, to_z)]
    column_late = after(column, *late[1], *to_z, opposites[2])
    over_x, over_y = shift(column_late, "x", 1), shift(column_late, "y", 1)
    along_z[0] = after(along_z[0], corner)
    state, grad = simple(
        lambda *refs: state_body(order, rows, len(groups[1]) - 1, *refs),
        [((3, rows, width), low), ((rows, width), full)],
        *cores, *came[1], *late[1], master, moment_one, moment_two, *along_z,
    )

    pieces, where = [], []
    for fy, fx, piece in ((0, 0, column), (1, 1, corner), (0, 1, over_x), (1, 0, over_y)):
        pieces += [piece, shift(piece, "c", 1)]
        where += [[(by, fy, fx, fc) for by in range(planes)] for fc in (0, 1)]
    keys, input_grad = pl.pallas_call(
        lambda *refs: both_ways_body(planes, rows, where, *refs),
        out_shape=[
            jax.ShapeDtypeStruct((many, width), low),
            jax.ShapeDtypeStruct((many, features), low),
        ],
        in_specs=[VMEM] * (3 + len(pieces)),
        out_specs=[VMEM, pl.BlockSpec(memory_space=pltpu.HBM)],
        scratch_shapes=[
            pltpu.VMEM((many, features), low),
            pltpu.SemaphoreType.DMA((2 * planes,)),
        ],
        cost_estimate=pl.CostEstimate(flops=8, bytes_accessed=8, transcendentals=0),
        compiler_params=pltpu.CompilerParams(vmem_limit_bytes=24 * MIB),
    )(tokens, key_grad, rstd, *pieces)

    beside = shift(state, "c", 1)
    across = shift(after(state, beside), "x", 1)
    new_master, new_one, new_two = simple(
        update_body, [((rows, width), full)] * 3, grad, master, moment_one, moment_two
    )
    diagonal = shift(after(across, keys, new_one), "c", 1)
    new_weight, held = simple(
        lambda *refs: finish_body(rows, *refs),
        [(weight.shape, low), ((3, rows, width), full)],
        buddy, state, beside, across, diagonal,
        scalars=1,
    )
    return (keys, input_grad, new_weight, new_master, new_one, new_two, held)


def solution(mesh):
    members, domains = mesh.devices.shape
    split = Mesh(mesh.devices.reshape(members // 2, 2, domains // 2, 2), ("z", "y", "x", "c"))
    every = ("z", "y", "x", "c")
    placed = (
        P(every, None),
        P(every, None),
        P(("z", "y"), None),
        P(every, None),
        P(every, None),
        P(every, None),
        P(),
        P(),
    )
    return jax.shard_map(
        on_device,
        mesh=split,
        in_specs=placed,
        out_specs=(
            P(every, None),
            P(every, None),
            P(("z", "y"), None),
            P(every, None),
            P(every, None),
            P(every, None),
            P(None, every, None),
        ),
        check_vma=False,
    )
```

```python
import jax
import jax.numpy as jnp
from jax import lax
from jax.experimental import pallas as pl
from jax.experimental.pallas import tpu as pltpu
from jax.sharding import Mesh
from jax.sharding import PartitionSpec as P

STEP = 100


def shift(value, axis, by):
    size = lax.axis_size(axis)
    return lax.ppermute(value, axis, [(i, (i + by) % size) for i in range(size)])


def pick(array, index, dim):
    return lax.dynamic_index_in_dim(array, index, dim, keepdims=False)


def scatter_sum(terms, axis, dim):
    size = lax.axis_size(axis)
    here = lax.axis_index(axis)
    arrived = [
        shift(pick(terms, (here + by) % size, dim).astype(jnp.bfloat16), axis, by)
        for by in range(1, size)
    ]
    total = pick(terms, here, dim)
    for term in arrived:
        total = total + term.astype(jnp.float32)
    return total


def gather(value, axis, dim):
    size = lax.axis_size(axis)
    here = lax.axis_index(axis)
    if size == 2:
        other = shift(value, axis, 1)
        first = jnp.where(here == 0, value, other)
        second = jnp.where(here == 0, other, value)
        return jnp.stack((first, second), axis=dim)
    slots = jnp.zeros(value.shape[:dim] + (size,) + value.shape[dim:], value.dtype)
    for by in range(size):
        arrived = shift(value, axis, by) if by else value
        slots = lax.dynamic_update_index_in_dim(slots, arrived, (here - by) % size, dim)
    return slots


def general(tokens, key_grad, weight, master, moment_one, moment_two, live, buddy):
    planes, rows_of, chips, cores = (lax.axis_size(a) for a in ("z", "y", "x", "c"))
    z, y, x, c = (lax.axis_index(a) for a in ("z", "y", "x", "c"))
    member = z * rows_of + y
    domain = x * cores + c
    rows, width = master.shape
    half = rows // 2
    features = tokens.shape[1]

    xf = tokens.astype(jnp.float32)
    rstd = lax.rsqrt(jnp.mean(xf * xf, axis=1, keepdims=True) + 1e-05)
    hat = xf * rstd
    normed = hat.astype(jnp.bfloat16)

    quarter = pick(pick(weight.reshape(chips, cores, rows, width), x, 0), c, 0)
    column = gather(quarter, "z", 0)
    upper = gather(gather(column[:, :half], "y", 1), "x", 2)
    lower = gather(gather(column[:, half:], "x", 1), "y", 1)
    mine = jnp.concatenate((upper, lower), axis=3)
    whole = gather(mine, "c", 3).reshape(features, width)

    live_float = live.astype(jnp.float32)
    norming = live.shape[0] * live.shape[1] / (jnp.sum(live_float) * tokens.shape[0])
    alive_here = pick(pick(live_float, member, 0), domain, 0)
    scale = alive_here * norming
    product = lax.dot_general(
        normed, key_grad, (((0,), (0,)), ((), ())), preferred_element_type=jnp.float32
    )
    terms = (product * scale).reshape(planes, rows_of, chips, cores, rows, width)
    terms = scatter_sum(terms, "c", 3)
    upper_sum = scatter_sum(scatter_sum(terms[:, :, :, :half], "x", 2), "y", 1)
    lower_sum = scatter_sum(scatter_sum(terms[:, :, :, half:], "y", 1), "x", 1)
    grad = scatter_sum(jnp.concatenate((upper_sum, lower_sum), axis=1), "z", 0)

    new_one = 0.9 * moment_one + 0.1 * grad
    new_two = 0.95 * moment_two + 0.05 * grad * grad
    first = 1.0 - 0.9**STEP
    second = 1.0 - 0.95**STEP
    update = new_one / first / (jnp.sqrt(new_two / second) + 1e-08)
    new_master = master - 0.002 * (update + 0.1 * master)

    state = jnp.stack((new_master, new_one, new_two)).astype(jnp.bfloat16)
    states = gather(state, "x", 0)
    new_weight = gather(states[:, 0], "c", 1).reshape(weight.shape)
    slots = jnp.arange(chips * cores, dtype=jnp.int32)
    source = jnp.sum(slots * (buddy == domain).astype(jnp.int32))
    other_source = jnp.sum(slots * (buddy == x * cores + 1 - c).astype(jnp.int32))
    from_core = shift(pick(states, other_source // cores, 0), "c", 1)
    from_column = pick(states, source // cores, 0)
    held = jnp.where(source % cores == c, from_column, from_core).astype(jnp.float32)

    keys = jnp.dot(normed, whole, preferred_element_type=jnp.float32)
    inner = jnp.sum(key_grad.astype(jnp.float32) * keys, axis=1, keepdims=True) / features
    back = lax.dot_general(
        key_grad, whole, (((1,), (1,)), ((), ())), preferred_element_type=jnp.float32
    )
    input_grad = (rstd * (back - hat * inner)).astype(jnp.bfloat16)
    return (keys.astype(jnp.bfloat16), input_grad, new_weight, new_master, new_one, new_two, held)


VMEM = pl.BlockSpec(memory_space=pltpu.VMEM)
SMEM = pl.BlockSpec(memory_space=pltpu.SMEM)
MIB = 2**20


def local(body, outs, flops, traffic, limit, *operands, scalars=0, **more):
    return pl.pallas_call(
        body,
        out_shape=[jax.ShapeDtypeStruct(s, t) for s, t in outs],
        in_specs=[SMEM] * scalars + [VMEM] * (len(operands) - scalars),
        out_specs=[VMEM] * len(outs),
        cost_estimate=pl.CostEstimate(flops=8, bytes_accessed=8, transcendentals=0),
        compiler_params=pltpu.CompilerParams(vmem_limit_bytes=limit * MIB),
        **more,
    )(*operands)


def after(value, *others):
    return lax.optimization_barrier((value, *others))[0]


def place():
    return tuple(lax.axis_index(a) for a in ("z", "y", "x", "c"))


def block_of(planes, by, flip_y, flip_x):
    z, y, x, _ = place()
    z = lax.rem(z + (by + planes) % planes, planes)
    return (z * 2 + (1 - y if flip_y else y)) * 2 + (1 - x if flip_x else x)


def prepare_body(rows, order, tokens, ours, soon, later, rstd_out, held, sems):
    c = lax.axis_index("c")
    many, features = tokens.shape
    step = many // 8

    def rows_in(i):
        span = pl.ds(pl.multiple_of(i * step, step), step)
        return pltpu.make_async_copy(tokens.at[span], held.at[span], sems.at[i])

    for i in range(8):
        rows_in(i).start()
    places = [(by, fy, fx) for by in order for fy in (0, 1) for fx in (0, 1)]

    def part(i, _):
        rows_in(i).wait()
        span = pl.ds(pl.multiple_of(i * step, step), step)
        squares = jnp.zeros((step, 128), jnp.float32)
        for j in range(0, features, 512):
            some = held[span, j : j + 512].astype(jnp.float32)
            some = some * some
            for k in range(0, 512, 128):
                squares = squares + some[:, k : k + 128]
        mean = jnp.sum(squares, axis=1, keepdims=True) / features
        rstd = lax.rsqrt(mean + 1e-05)
        rstd_out[span] = rstd
        for side, outs in ((1 - c, (soon, later)), (c, (ours,))):
            share = len(places) // len(outs)
            for j, flips in enumerate(places):
                start = (block_of(len(order), *flips) * 2 + side) * rows
                columns = pl.ds(pl.multiple_of(start, rows), rows)
                at = j % share * rows
                outs[j // share][span, at : at + rows] = (
                    held[span, columns].astype(jnp.float32) * rstd
                ).astype(jnp.bfloat16)
        return 0

    lax.fori_loop(0, 8, part, 0)


def prepare(tokens, rows, order):
    many, features = tokens.shape
    side = ((many, features // 2), jnp.bfloat16)
    part = ((many, features // 4), jnp.bfloat16)
    return pl.pallas_call(
        lambda *refs: prepare_body(rows, order, *refs),
        out_shape=[jax.ShapeDtypeStruct(s, t) for s, t in (side, part, part, ((many, 1), jnp.float32))],
        in_specs=[pl.BlockSpec(memory_space=pltpu.HBM)],
        out_specs=[VMEM] * 4,
        scratch_shapes=[pltpu.VMEM(tokens.shape, tokens.dtype), pltpu.SemaphoreType.DMA((8,))],
        cost_estimate=pl.CostEstimate(flops=8, bytes_accessed=8, transcendentals=0),
        compiler_params=pltpu.CompilerParams(vmem_limit_bytes=47 * MIB),
    )(tokens)


def flags_body(many, live, flags):
    z, y, x, c = place()
    for row, core in ((0, c), (8, 1 - c)):
        alive = live[x * 2 + core, z * 2 + y]
        flags[row : row + 8] = jnp.full((8, flags.shape[1]), alive).astype(jnp.float32)
    blocks = live.shape[0] * live.shape[1]
    alive = sum(live[i, j] for i in range(live.shape[0]) for j in range(live.shape[1]))
    flags[16:24] = blocks / (jnp.full((8, flags.shape[1]), alive).astype(jnp.float32) * many)


def product(order, by, flip_y, flip_x, lower, rows, cores):
    half = rows // 2
    start = (order.index(by) * 4 + flip_y * 2 + flip_x) * rows + lower * half

    def term(parts, grad, flag):
        share = len(order) * 4 * rows // len(parts)
        at = start % share
        return flag * lax.dot_general(
            parts[start // share][:, at : at + half],
            grad[...],
            (((0,), (0,)), ((), ())),
            preferred_element_type=jnp.float32,
        )

    return sum(term(*core) for core in cores)


def first_body(order, rows, group, flags, ours, theirs, own_grad, their_grad, to_x, to_y):
    cores = (((ours,), own_grad, flags[0:1]), ((theirs, theirs), their_grad, flags[8:9]))
    for i, by in enumerate(group):
        for flip in (0, 1):
            to_x[flip, i] = product(order, by, flip, 1, 0, rows, cores).astype(jnp.bfloat16)
            to_y[flip, i] = product(order, by, 1, flip, 1, rows, cores).astype(jnp.bfloat16)


def second_body(order, rows, group, flags, ours, soon, later, own_grad, their_grad, from_x, from_y, to_y, to_x):
    cores = (((ours,), own_grad, flags[0:1]), ((soon, later), their_grad, flags[8:9]))
    for i, by in enumerate(group):
        upper = product(order, by, 1, 0, 0, rows, cores)
        to_y[i] = (upper + from_x[1, i].astype(jnp.float32)).astype(jnp.bfloat16)
        lower = product(order, by, 0, 1, 1, rows, cores)
        to_x[i] = (lower + from_y[1, i].astype(jnp.float32)).astype(jnp.bfloat16)


def own_half(order, rows, by, i, lower, cores, near, second):
    total = product(order, by, 0, 0, lower, rows, cores)
    return total + near[0, i].astype(jnp.float32) + second[i].astype(jnp.float32)


def third_body(order, rows, group, flags, ours, soon, later, own_grad, their_grad, from_x, from_y, late_y, late_x, *outs):
    cores = (((ours,), own_grad, flags[0:1]), ((soon, later), their_grad, flags[8:9]))
    half = rows // 2
    for i, by in enumerate(group):
        upper = own_half(order, rows, by, i, 0, cores, from_x, late_y)
        lower = own_half(order, rows, by, i, 1, cores, from_y, late_x)
        outs[i][:half] = upper.astype(jnp.bfloat16)
        outs[i][half:] = lower.astype(jnp.bfloat16)


def stepped(grad, master, moment_one, moment_two):
    one = 0.9 * moment_one + 0.1 * grad
    two = 0.95 * moment_two + 0.05 * grad * grad
    first = 1.0 - 0.9**STEP
    second = 1.0 - 0.95**STEP
    update = one / first / (jnp.sqrt(two / second) + 1e-08)
    return master - 0.002 * (update + 0.1 * master), one, two


def state_body(order, rows, at, flags, ours, soon, later, own_grad, their_grad, from_x, from_y, late_y, late_x, master, moment_one, moment_two, *rest):
    *along_z, state, grad = rest
    cores = (((ours,), own_grad, flags[0:1]), ((soon, later), their_grad, flags[8:9]))
    half = rows // 2
    for lower, near, second in ((0, from_x, late_y), (1, from_y, late_x)):
        total = own_half(order, rows, 0, at, lower, cores, near, second)
        span = pl.ds(lower * half, half)
        for term in along_z:
            total = total + term[span].astype(jnp.float32)
        total = total * flags[16:17]
        grad[span] = total
        for i, value in enumerate(stepped(total, master[span], moment_one[span], moment_two[span])):
            state[i, span] = value.astype(jnp.bfloat16)


def update_body(grad, master, moment_one, moment_two, new_master, new_one, new_two):
    new_master[...], new_one[...], new_two[...] = stepped(
        grad[...], master[...], moment_one[...], moment_two[...]
    )


def piece_columns(planes, rows, by, flip_y, flip_x, flip_c):
    c = lax.axis_index("c")
    block = block_of(planes, -by, flip_y, flip_x)
    return pl.ds(pl.multiple_of((block * 2 + (1 - c if flip_c else c)) * rows, rows), rows)


def normed_at(tokens, span, rstd):
    return (tokens[:, span].astype(jnp.float32) * rstd).astype(jnp.bfloat16)


def each(where, pieces):
    for blocks, piece in zip(where, pieces):
        for k, at in enumerate(blocks):
            yield at, piece.at[k]


def add_keys(planes, rows, where, tokens, rstd, pieces, keys):
    for blocks, piece in zip(where, pieces):
        normed = [normed_at(tokens, piece_columns(planes, rows, *at), rstd) for at in blocks]
        deep = piece[...].reshape(-1, piece.shape[2])
        keys = keys + jnp.dot(
            jnp.concatenate(normed, axis=1), deep, preferred_element_type=jnp.float32
        )
    return keys


def back_of(key_grad, piece):
    return lax.dot_general(
        key_grad[...], piece[...], (((1,), (1,)), ((), ())), preferred_element_type=jnp.float32
    )


def both_ways_body(planes, rows, where, tokens, key_grad, rstd_in, *rest):
    pieces = rest[: len(where)]
    keys_out, input_grad, made, sems = rest[len(where) :]
    features = tokens.shape[1]
    rstd = rstd_in[...]
    keys = jnp.zeros(key_grad.shape, jnp.float32)
    keys = add_keys(planes, rows, where, tokens, rstd, pieces, keys)
    keys_out[...] = keys.astype(jnp.bfloat16)
    inner = jnp.sum(key_grad[...].astype(jnp.float32) * keys, axis=1, keepdims=True) / features
    slope = jnp.broadcast_to(rstd * rstd * inner, (tokens.shape[0], rows))
    found = dict(each(where, pieces))
    copies = []
    for i, (fy, by) in enumerate((fy, by) for fy in (0, 1) for by in range(planes)):
        for at in ((by, fy, fx, fc) for fx in (0, 1) for fc in (0, 1)):
            span = piece_columns(planes, rows, *at)
            back = rstd * back_of(key_grad, found[at])
            made[:, span] = (back - tokens[:, span].astype(jnp.float32) * slope).astype(jnp.bfloat16)
        start = block_of(planes, -by, fy, 0) // 2 * (4 * rows)
        span = pl.ds(pl.multiple_of(start, rows), 4 * rows)
        copies.append(pltpu.make_async_copy(made.at[:, span], input_grad.at[:, span], sems.at[i]))
        copies[-1].start()
    for copy in copies:
        copy.wait()


def quarter_body(rows, weight, out):
    _, _, x, c = place()
    out[...] = weight[pl.ds(pl.multiple_of((x * 2 + c) * rows, rows), rows)]


def stack_body(*refs):
    *parts, out = refs
    for i, part in enumerate(parts):
        out[i] = part[...]


def finish_body(rows, buddy, own, beside, across, diagonal, new_weight, held):
    _, _, x, c = place()
    domain = x * 2 + c
    for flip_x, flip_c, state in ((0, 0, own), (0, 1, beside), (1, 0, across), (1, 1, diagonal)):
        sender = (1 - x if flip_x else x) * 2 + (1 - c if flip_c else c)
        new_weight[pl.ds(pl.multiple_of(sender * rows, rows), rows)] = state[0]

        @pl.when(buddy[sender] == domain)
        def _():
            held[...] = state[...].astype(jnp.float32)


def on_device(tokens, key_grad, weight, master, moment_one, moment_two, live, buddy):
    planes, rows_of, chips, cores = (lax.axis_size(a) for a in ("z", "y", "x", "c"))
    rows, width = master.shape
    many, features = tokens.shape
    if (rows_of, chips, cores) != (2, 2, 2) or rows % 256 or many % 128 or planes < 2 or width != 512:
        return general(tokens, key_grad, weight, master, moment_one, moment_two, live, buddy)
    half = rows // 2
    low, full = jnp.bfloat16, jnp.float32
    live = live.T
    order = sorted(range(1, planes), key=lambda by: min(by, planes - by)) + [0]

    def simple(body, outs, *operands, limit=12, **more):
        return local(body, outs, 8, 8, limit, *operands, **more)

    ours, soon, later, rstd = prepare(tokens, rows, order)
    flags, = simple(
        lambda *refs: flags_body(many, *refs),
        [((24, width), full)],
        after(live, soon),
        scalars=1,
    )
    grads = key_grad, shift(after(key_grad, soon), "c", 1)
    theirs = shift(soon, "c", 1), shift(after(later, grads[1]), "c", 1)
    cores = (flags, ours, *theirs, *grads)

    groups = order[: planes // 2], order[planes // 2 :]
    came, made = [], []
    for group, part in zip(groups, theirs):
        to_x, to_y = simple(
            lambda *refs: first_body(order, rows, group, *refs),
            [((2, len(group), half, width), low)] * 2,
            flags, ours, part, *grads,
        )
        made.append(to_x)
        came.append((shift(to_x, "x", 1), shift(to_y, "y", 1)))
    quarter, = simple(lambda *refs: quarter_body(rows, *refs), [((rows, width), low)], after(weight, made[0]))
    opposite = lax.ppermute(quarter, ("y", "x"), [(0, 3), (1, 2), (2, 1), (3, 0)])
    quarters, opposites = [quarter], [opposite]
    for by in range(1, planes):
        quarters.append(shift(quarters[-1], "z", 1))
        opposites.append(shift(opposites[-1], "z", 1))
    column, = simple(
        stack_body,
        [((planes, rows, width), low)],
        *quarters,
    )
    corner, = simple(stack_body, [((planes, rows, width), low)], *opposites)

    late = []
    along_z = []
    first_out = ()
    for group, (from_x, from_y), ties in zip(groups, came, (quarters[1:3], ())):
        to_y, to_x = simple(
            lambda *refs: second_body(order, rows, group, *refs),
            [((len(group), half, width), low)] * 2,
            *cores, after(from_x, *(late_out if along_z else ())), after(from_y, *ties),
        )
        late_out = (to_y, to_x)
        late.append((shift(to_y, "y", 1), shift(to_x, "x", 1)))
        sent = [by for by in group if by]
        to_z = simple(
            lambda *refs: third_body(order, rows, sent, *refs),
            [((rows, width), low)] * len(sent),
            *cores, from_x, from_y, after(late[-1][0], *(first_out or (*quarters[3:], opposites[1]))), late[-1][1],
        )
        first_out = to_z
        along_z += [shift(term, "z", by) for by, term in zip(sent, to_z)]
    column_late = after(column, *late[1], *to_z, opposites[2])
    over_x, over_y = shift(column_late, "x", 1), shift(column_late, "y", 1)
    along_z[0] = after(along_z[0], corner)
    state, grad = simple(
        lambda *refs: state_body(order, rows, len(groups[1]) - 1, *refs),
        [((3, rows, width), low), ((rows, width), full)],
        *cores, *came[1], *late[1], master, moment_one, moment_two, *along_z,
    )

    beside = shift(state, "c", 1)
    across = shift(state, "x", 1)
    pieces, where = [], []
    for fy, fx, piece in ((0, 0, column), (1, 1, corner), (0, 1, over_x), (1, 0, over_y)):
        fetched = piece is over_x or piece is over_y
        pieces += [piece, shift(after(piece, beside) if fetched else piece, "c", 1)]
        where += [[(by, fy, fx, fc) for by in range(planes)] for fc in (0, 1)]
    keys, input_grad = pl.pallas_call(
        lambda *refs: both_ways_body(planes, rows, where, *refs),
        out_shape=[
            jax.ShapeDtypeStruct((many, width), low),
            jax.ShapeDtypeStruct((many, features), low),
        ],
        in_specs=[VMEM] * (3 + len(pieces)),
        out_specs=[VMEM, pl.BlockSpec(memory_space=pltpu.HBM)],
        scratch_shapes=[
            pltpu.VMEM((many, features), low),
            pltpu.SemaphoreType.DMA((2 * planes,)),
        ],
        cost_estimate=pl.CostEstimate(flops=8, bytes_accessed=8, transcendentals=0),
        compiler_params=pltpu.CompilerParams(vmem_limit_bytes=24 * MIB),
    )(tokens, key_grad, rstd, *pieces)

    new_master, new_one, new_two = simple(
        update_body, [((rows, width), full)] * 3, grad, master, moment_one, moment_two
    )
    diagonal = shift(after(across, keys, new_one), "c", 1)
    new_weight, held = simple(
        lambda *refs: finish_body(rows, *refs),
        [(weight.shape, low), ((3, rows, width), full)],
        buddy, state, beside, across, diagonal,
        scalars=1,
    )
    return (keys, input_grad, new_weight, new_master, new_one, new_two, held)


def solution(mesh):
    members, domains = mesh.devices.shape
    split = Mesh(mesh.devices.reshape(members // 2, 2, domains // 2, 2), ("z", "y", "x", "c"))
    every = ("z", "y", "x", "c")
    placed = (
        P(every, None),
        P(every, None),
        P(("z", "y"), None),
        P(every, None),
        P(every, None),
        P(every, None),
        P(),
        P(),
    )
    return jax.shard_map(
        on_device,
        mesh=split,
        in_specs=placed,
        out_specs=(
            P(every, None),
            P(every, None),
            P(("z", "y"), None),
            P(every, None),
            P(every, None),
            P(every, None),
            P(None, every, None),
        ),
        check_vma=False,
    )
```
